256 devices in a mesh: replica: 16 (over z_lo, x, core), tensor: 16 (over z_hi, y).
Axes of the slice: x: 4, y: 4, z: 8 (z_hi: 4, z_lo: 2; z = z_hi * 2 + z_lo), core: 2. Of those that a mesh axis runs over, the one named last changes fastest.
Arguments:
- grads: bfloat16 [16, 4096, 8192], P('replica', None, 'tensor'), may hold values from -100 to 100
- exponents: int32 [16, 64], P('replica', 'tensor'), may hold values from -4 to 1
- signs: int32 [4096], replicated, may hold values from 0 to 1
- weights: bfloat16 [4096, 8192], P(None, 'tensor'), may hold values from -3 to 3
Outputs:
- new_weights: bfloat16 [4096, 8192], P(None, 'tensor')
The draws below stay inside these ranges and needn't reach their ends.
All inputs are finite; a program needn't handle non-finite values.
Results may differ from the reference program's by a relative error of at most 0.015.
Values may be sent and summed in bfloat16 or wider, within the bound.
A program may use at most 64 MiB of HBM per device.

```python
import math
import jax
import jax.numpy as jnp
from jax import lax

COLS = 8192
ROWS = 4096
GROUP = 128
N_REPLICA = 16


def draw_grads(key, part):
    key = jax.random.fold_in(key, 11)
    own_key = jax.random.fold_in(key, 1)
    rough_key = jax.random.fold_in(key, 3)
    position = jnp.arange(COLS, dtype=jnp.float32) / (COLS - 1)
    rough = jax.random.uniform(rough_key, (COLS,), jnp.float32, 0.7, 1.4)
    values = jnp.clip(jax.random.normal(own_key, (N_REPLICA, ROWS, COLS), jnp.float32), -6.0, 6.0)
    col_scale = jnp.exp(jnp.log(3.0) * position) * rough
    return (values * col_scale[None, None, :]).astype(jnp.bfloat16)


def plant(values, rng, low, top_value):
    dims = values.shape
    place = [jax.random.randint(jax.random.fold_in(rng, axis), (), 0, dims[axis]) for axis in range(len(dims))]
    values = values.at[tuple(place)].set(low)
    longest = dims.index(max(dims))
    place[longest] = (place[longest] + 1) % dims[longest]
    return values.at[tuple(place)].set(top_value)


def shard_levels(stream_key, extent, shards, least, top_value):
    level, own = 1.0, jax.random.fold_in(stream_key, 6)
    for dim, blocks in shards:
        draws = jnp.exp(jax.random.uniform(jax.random.fold_in(own, dim), (blocks,), jnp.float32, least / len(shards), top_value / len(shards)))
        level = level * jnp.repeat(draws, extent[dim] // blocks).reshape([-1 if axis == dim else 1 for axis in range(len(extent))])
    return level


def noise(key, extent, scale, limit, split=(), kind=jnp.bfloat16):
    drawn = scale * jax.random.normal(key, extent, jnp.float32)
    if split:
        drawn = drawn * shard_levels(key, extent, split, -0.22, 0.18)
    return jnp.clip(drawn, -limit, limit).astype(kind)


def setup_inputs(seed: int = 0) -> dict:
    splits = jax.random.split(jax.random.key(seed), 5)
    grads = draw_grads(jax.random.fold_in(splits[4], 71), 0)
    exponents = plant(jax.random.randint(splits[1], (N_REPLICA, COLS // GROUP), -4, 2), jax.random.fold_in(splits[1], 1), -4, 1).astype(jnp.int32)
    signs = plant(jax.random.randint(splits[2], (ROWS,), 0, 2), jax.random.fold_in(splits[2], 1), 0, 1).astype(jnp.int32)
    weights = noise(splits[3], (ROWS, COLS), 0.5, 3.0, ((1, 16),))
    return dict(grads=grads, exponents=exponents, signs=signs, weights=weights)


def hadamard(side_len):
    index_row = jnp.arange(side_len, dtype=jnp.int32)[:, None]
    index_col = jnp.arange(side_len, dtype=jnp.int32)[None, :]
    parity = jnp.zeros((side_len, side_len), jnp.int32)
    for bit_pos in range(side_len.bit_length()):
        parity = parity + (index_row >> bit_pos & 1) * (index_col >> bit_pos & 1)
    return (1 - 2 * (parity % 2)).astype(jnp.float32) / math.sqrt(side_len)

def power_of_two(exponent_vals):
    values = jnp.zeros(exponent_vals.shape, jnp.float32)
    for power in range(-4, 2):
        values = jnp.where(exponent_vals == power, jnp.float32(2.0 ** power), values)
    return values

def rotate(matrix_in, hadamard_table):
    side_len = hadamard_table.shape[0]
    columns = matrix_in.shape[1]
    reshaped = matrix_in.astype(jnp.float32).reshape(side_len, side_len, columns)
    inner_pass = jnp.einsum('jb,abc->ajc', hadamard_table, reshaped, precision=lax.Precision.HIGHEST)
    outer_pass = jnp.einsum('ia,ajc->ijc', hadamard_table, inner_pass, precision=lax.Precision.HIGHEST)
    return outer_pass.reshape(side_len * side_len, columns)

def reference(grads, exponents, signs, weights):
    hadamard_table = hadamard(math.isqrt(ROWS))
    sign_col = (2 * signs - 1).astype(jnp.float32)[:, None]
    col_scales = jnp.repeat(power_of_two(exponents), GROUP, axis=1)

    def accumulate(summed, pieces):
        grad_one, scale_one = pieces
        rotated = rotate(grad_one.astype(jnp.float32) * sign_col, hadamard_table)
        quantized = jnp.clip(rotated / scale_one[None, :], -4.0, 4.0).astype(jnp.bfloat16)
        return (summed + quantized.astype(jnp.float32) * scale_one[None, :], None)
    summed, unused = lax.scan(accumulate, jnp.zeros((ROWS, COLS), jnp.float32), (grads, col_scales))
    sum_squares = jnp.sum(summed * summed)
    root_mean = jnp.sqrt(sum_squares / (ROWS * COLS) + 1e-06)
    factor = 0.5 / root_mean
    unrotated = rotate(summed, hadamard_table) * sign_col
    return (weights.astype(jnp.float32) - factor * unrotated).astype(jnp.bfloat16)
```

```python
import functools

import jax
import jax.numpy as jnp
from jax import lax
from jax.experimental import pallas as pl
from jax.experimental.pallas import tpu as pltpu
from jax.sharding import PartitionSpec as P

COLS = 8192
OUTER, INNER = 16, 256
LANES = 128
NX, NA1 = 4, 6
MESH = pl.DeviceIdType.MESH


def hadamard_values(values):
    values = list(values)
    step = 1
    while step < len(values):
        for i in range(len(values)):
            if not i & step:
                u, v = values[i], values[i + step]
                values[i], values[i + step] = u + v, u - v
        step *= 2
    return values


def kernel(nt, exps, signs, grads, weights, out, g, w, y, hf, hb, qp, pr, p, rx1, s1, rz1, rz2, d, rx2, gv, ar, ld, ss, rs):
    f32, bf16 = jnp.float32, jnp.bfloat16
    r, t = lax.axis_index("replica"), lax.axis_index("tensor")
    z, x, c = r // 8, (r // 2) % 4, r % 2
    zh, yy = t // 4, t % 4
    oz, oc = 1 - z, 1 - c

    def dev(z=z, x=x, c=c, zh=zh, yy=yy):
        return (z * 8 + x * 2 + c, zh * 4 + yy)

    def xo(j):
        return lax.rem(x + j, 4)

    xpeer = {j: dev(x=xo(j)) for j in (1, 2, 3)}
    zpeer, cpeer, zcpeer = dev(z=oz), dev(c=oc), dev(z=oz, c=oc)
    ypeer = {j: dev(yy=lax.rem(yy + j, 4)) for j in (1, 2, 3)}
    zhpeer = {j: dev(zh=lax.rem(zh + j, 4)) for j in (1, 2, 3)}
    peers = [*xpeer.values(), zpeer, cpeer, zcpeer]
    if nt > 1:
        peers += [*ypeer.values(), *zhpeer.values()]
    barrier = pltpu.get_barrier_semaphore()
    for peer in peers:
        pl.semaphore_signal(barrier, inc=1, device_id=peer, device_id_type=MESH)

    order = [(0, oc), (0, c), (1, oc), (1, c)]
    loads = []
    for n, (k, half) in enumerate(order):
        cols = pl.ds(pl.multiple_of((2 * half + k) * LANES, LANES), LANES)
        loads.append(pltpu.make_async_copy(grads.at[:, :, cols], g.at[n], ld.at[n]))
        loads[-1].start()
    wloads = [
        pltpu.make_async_copy(weights.at[:, :, pl.ds(n * LANES, LANES)], w.at[n], ld.at[4 + n]) for n in range(4)
    ]

    sent = []

    def remote(src, dst, peer):
        i = len(sent)
        copy = pltpu.make_async_remote_copy(
            src_ref=src, dst_ref=dst, send_sem=ss.at[i], recv_sem=rs.at[i], device_id=peer, device_id_type=MESH
        )
        copy.start()
        sent.append(copy)
        return copy

    row = lax.broadcasted_iota(jnp.int32, (INNER, INNER), 0)
    col = lax.broadcasted_iota(jnp.int32, (INNER, INNER), 1)
    v = row & col
    v = v ^ (v >> 4)
    v = v ^ (v >> 2)
    v = v ^ (v >> 1)
    table = (1 - 2 * (v & 1)).astype(f32) * (1.0 / 64.0)

    def sign_row(a):
        return (2 * signs[pl.ds(a, 1), :] - 1).astype(f32)

    def build_forward(a, carry):
        hf[a] = (table * sign_row(a)).astype(bf16)
        return carry

    lax.fori_loop(0, OUTER, build_forward, 0)

    def build_back():
        table16 = table.astype(bf16)

        def one(a, carry):
            diagonal = jnp.where(row == col, jnp.broadcast_to(sign_row(a), (INNER, INNER)), 0.0).astype(bf16)
            hb[a] = jnp.dot(diagonal, table16, preferred_element_type=f32).astype(bf16)
            return carry

        lax.fori_loop(0, OUTER, one, 0)

    def inner_pass(n):
        loads[n].wait()

        def one(a, carry):
            y[a] = jnp.dot(hf[a], g[n, a], preferred_element_type=f32)
            return carry

        lax.fori_loop(0, OUTER, one, 0)

    def outer_pass(n, dst, other=None):
        k, half = order[n]
        e = exps[0, 2 * half + k]
        top = jnp.float32(0.0)
        for power in range(-4, 2):
            top = jnp.where(e == power, jnp.float32(4.0 * 2.0**power), top)

        def one(i, carry):
            for part in (0, 16):
                rows = pl.ds(pl.multiple_of(i * 32 + part, 16), 16)
                values = hadamard_values([y[a, rows, :] for a in range(OUTER)])
                for a in range(OUTER):
                    q = jnp.clip(values[a], -top, top).astype(bf16)
                    at = (a, i // 2, i % 2, pl.ds(part, 16))
                    if other is not None:
                        q = (q.astype(f32) + other[at].astype(f32)).astype(bf16)
                    dst[at] = q
            return carry

        lax.fori_loop(0, 8, one, 0)

    pair, c_a1x, c_a2z, c_a1z, c_a2x = {}, {}, {}, {}, {}
    for k in (0, 1):
        inner_pass(2 * k)
        outer_pass(2 * k, qp.at[k])
        if k == 0:
            pl.semaphore_wait(barrier, len(peers))
        pair[k] = remote(qp.at[k], pr.at[k], cpeer)
        inner_pass(2 * k + 1)
        pair[k].wait_recv()
        outer_pass(2 * k + 1, p.at[k], pr.at[k])
        c_a2z[k] = remote(p.at[k, pl.ds(NA1, OUTER - NA1), :, oz], rz2.at[k], zpeer)
        c_a1x[k] = [
            remote(p.at[k, pl.ds(0, NA1), xo(j)], rx1.at[k, j - 1], xpeer[j]) for j in (2, 1, 3)
        ]
    for load in wloads:
        load.start()
    build_back()

    for k in (0, 1):
        for copy in c_a1x[k]:
            copy.wait_recv()

        def add_x(a, carry, k=k):
            total = p[k, a, x].astype(f32)
            for j in range(3):
                total = total + rx1[k, j, a].astype(f32)
            s1[k, a] = total.astype(bf16)
            return carry

        lax.fori_loop(0, NA1, add_x, 0)
        c_a1z[k] = remote(s1.at[k, :, oz], rz1.at[k], zpeer)

        c_a2z[k].wait_recv()

        def add_z(a, carry, k=k):
            d[k, a] = (p[k, NA1 + a, :, z].astype(f32) + rz2[k, a].astype(f32)).astype(bf16)
            return carry

        lax.fori_loop(0, OUTER - NA1, add_z, 0)
        c_a2x[k] = [remote(d.at[k, :, xo(j)], rx2.at[k, j - 1], xpeer[j]) for j in (2, 1, 3)]

    own = {}
    squares = jnp.zeros((16, LANES), f32)
    for k in (0, 1):
        c_a1z[k].wait_recv()
        for copy in c_a2x[k]:
            copy.wait_recv()
        for part in (0, 16):
            rows = pl.ds(part, 16)
            values = []
            for a in range(OUTER):
                if a < NA1:
                    total = s1[k, a, z, rows, :].astype(f32) + rz1[k, a, rows, :].astype(f32)
                else:
                    total = d[k, a - NA1, x, rows, :].astype(f32)
                    for j in range(3):
                        total = total + rx2[k, j, a - NA1, rows, :].astype(f32)
                squares = squares + total * total
                values.append(total)
            values = hadamard_values(values)
            for a in range(OUTER):
                gv[2 * c + k, a, x, z, rows, :] = values[a].astype(bf16)
        piece = gv.at[2 * c + k, :, x, z]
        own[k] = {
            "z": remote(piece, piece, zpeer),
            "x": {j: remote(piece, piece, xpeer[j]) for j in (2, 1, 3)},
        }
        own[k]["c"] = [remote(piece, piece, cpeer)]

    rounds = [(x, xpeer), (2 * z + c, {2: zpeer, 1: cpeer, 3: zcpeer})]
    if nt > 1:
        rounds = [(yy, ypeer), (zh, zhpeer)] + rounds
    ar_state = {"value": squares[:8] + squares[8:]}

    def ar_send(n):
        slot, to = rounds[n]
        ar[n, slot] = ar_state["value"]
        ar_state["copies"] = [remote(ar.at[n, slot], ar.at[n, slot], to[j]) for j in (2, 1, 3)]

    def ar_recv(n):
        for copy in ar_state["copies"]:
            copy.wait_recv()
        ar_state["value"] = (ar[n, 0] + ar[n, 1]) + (ar[n, 2] + ar[n, 3])

    ar_send(0)
    done = 0
    for k in (0, 1):
        tile = 2 * c + k
        a1, a2 = pl.ds(0, NA1), pl.ds(NA1, OUTER - NA1)
        state = own[k]
        state["z"].wait_recv()
        second = gv.at[tile, a1, x, oz]
        relay_x = {j: remote(second, second, xpeer[j]) for j in (2, 1, 3)}
        whole = gv.at[tile, :, x, oz]
        state["c"].append(remote(whole, whole, cpeer))
        relay_z = {}
        for j in (1, 3, 2):
            state["x"][j].wait_recv()
            from_x = xo(4 - j)
            block = gv.at[tile, a2, from_x, z]
            relay_z[j] = remote(block, block, zpeer)
            whole = gv.at[tile, :, from_x, z]
            state["c"].append(remote(whole, whole, cpeer))
        if done < len(rounds):
            ar_recv(done)
            done += 1
            if done < len(rounds):
                ar_send(done)
        for j in (1, 3, 2):
            relay_x[j].wait_recv()
            relay_z[j].wait_recv()
            whole = gv.at[tile, :, xo(4 - j), oz]
            state["c"].append(remote(whole, whole, cpeer))
        if done < len(rounds):
            ar_recv(done)
            done += 1
            if done < len(rounds):
                ar_send(done)

    sum_squares = jnp.sum(jnp.sum(ar_state["value"], axis=0, keepdims=True), axis=1, keepdims=True)
    factor = 0.5 / jnp.sqrt(sum_squares / (OUTER * INNER * COLS) + 1e-06)
    for load in wloads:
        load.wait()

    stores = []

    def finish(tile):
        def one(a, carry):
            block = gv[tile, a].reshape(INNER, LANES)
            unrotated = jnp.dot(hb[a], block, preferred_element_type=f32)
            w[tile, a] = (w[tile, a].astype(f32) - factor * unrotated).astype(bf16)
            return carry

        lax.fori_loop(0, OUTER, one, 0)
        cols = pl.ds(pl.multiple_of(tile * LANES, LANES), LANES)
        copy = pltpu.make_async_copy(w.at[tile], out.at[:, :, cols], ld.at[8 + len(stores)])
        copy.start()
        stores.append(copy)

    for k in (0, 1):
        finish(2 * c + k)
        for copy in own[k]["c"]:
            copy.wait_recv()
        finish(2 * oc + k)
    for copy in stores:
        copy.wait()
    for copy in sent:
        copy.wait_send()


def body(exponents, signs, grads, weights, nt):
    bf16, f32 = jnp.bfloat16, jnp.float32
    na2 = OUTER - NA1
    n_copies = 2 * 27 + 3 * (4 if nt > 1 else 2)
    vmem = pltpu.VMEM
    columns = grads.shape[-1]
    full = (OUTER, NX, 2, 32, LANES)
    out = pl.pallas_call(
        functools.partial(kernel, nt),
        out_shape=jax.ShapeDtypeStruct((OUTER, INNER, columns), bf16),
        in_specs=[
            pl.BlockSpec(memory_space=pltpu.SMEM),
            pl.BlockSpec(memory_space=pltpu.VMEM),
            pl.BlockSpec(memory_space=pl.ANY),
            pl.BlockSpec(memory_space=pl.ANY),
        ],
        out_specs=pl.BlockSpec(memory_space=pl.ANY),
        scratch_shapes=[
            vmem((4, OUTER, INNER, LANES), bf16),
            vmem((4, OUTER, INNER, LANES), bf16),
            vmem((OUTER, INNER, LANES), f32),
            vmem((OUTER, INNER, INNER), bf16),
            vmem((OUTER, INNER, INNER), bf16),
            vmem((2, *full), bf16),
            vmem((2, *full), bf16),
            vmem((2, *full), bf16),
            vmem((2, 3, NA1, 2, 32, LANES), bf16),
            vmem((2, NA1, 2, 32, LANES), bf16),
            vmem((2, NA1, 32, LANES), bf16),
            vmem((2, na2, NX, 32, LANES), bf16),
            vmem((2, na2, NX, 32, LANES), bf16),
            vmem((2, 3, na2, 32, LANES), bf16),
            vmem((4, *full), bf16),
            vmem((4, 4, 8, LANES), f32),
            pltpu.SemaphoreType.DMA((12,)),
            pltpu.SemaphoreType.DMA((n_copies,)),
            pltpu.SemaphoreType.DMA((n_copies,)),
        ],
        compiler_params=pltpu.CompilerParams(
            collective_id=0, has_side_effects=True, vmem_limit_bytes=52 * 2**20
        ),
        name="average_step",
    )(
        exponents,
        signs.reshape(OUTER, INNER),
        grads.reshape(OUTER, INNER, columns),
        weights.reshape(OUTER, INNER, columns),
    )
    return out.reshape(OUTER * INNER, columns)


def solution(mesh):
    in_specs = (P("replica", None, "tensor"), P("replica", "tensor"), P(), P(None, "tensor"))
    nt = mesh.shape["tensor"]

    def step(grads, exponents, signs, weights):
        return body(exponents, signs, grads[0], weights, nt)

    return jax.shard_map(step, mesh=mesh, in_specs=in_specs, out_specs=P(None, "tensor"), check_vma=False)
```

```python
import functools

import jax
import jax.numpy as jnp
from jax import lax
from jax.experimental import pallas as pl
from jax.experimental.pallas import tpu as pltpu
from jax.sharding import PartitionSpec as P

COLS = 8192
OUTER, INNER = 16, 256
LANES, HALF = 128, 256
NA = 8
NG = 10
CHUNKS = [(0, 0), (0, 1), (1, 0), (1, 1)]
MESH = pl.DeviceIdType.MESH


def hadamard_values(values):
    values = list(values)
    step = 1
    while step < len(values):
        for i in range(len(values)):
            if not i & step:
                u, v = values[i], values[i + step]
                values[i], values[i + step] = u + v, u - v
        step *= 2
    return values


def inner_table():
    row = lax.broadcasted_iota(jnp.int32, (INNER, INNER), 0)
    col = lax.broadcasted_iota(jnp.int32, (INNER, INNER), 1)
    v = row & col
    v = v ^ (v >> 4)
    v = v ^ (v >> 2)
    v = v ^ (v >> 1)
    table = (1 - 2 * (v & 1)).astype(jnp.float32) * (1.0 / 64.0)
    return table.astype(jnp.bfloat16), row == col


def exchange(
    nt, exps_hbm, signs_hbm, grads, weights,
    gv, wv, hb, fac,
    exps, signs, g, y, qp, pr, p, rx1, s1, rz1, rz2, d, rx2, ov, ar, ld, ss, rs,
):
    f32, bf16 = jnp.float32, jnp.bfloat16
    r, t = lax.axis_index("replica"), lax.axis_index("tensor")
    z, x, c = r // 8, (r // 2) % 4, r % 2
    zh, yy = t // 4, t % 4
    oz, oc = 1 - z, 1 - c

    def dev(z=z, x=x, c=c, zh=zh, yy=yy):
        return (z * 8 + x * 2 + c, zh * 4 + yy)

    xo = {j: lax.rem(x + j, 4) for j in (1, 2, 3)}
    xpeer = {j: dev(x=xo[j]) for j in (1, 2, 3)}
    zpeer, cpeer, zcpeer = dev(z=oz), dev(c=oc), dev(z=oz, c=oc)
    ypeer = {j: dev(yy=lax.rem(yy + j, 4)) for j in (1, 2, 3)}
    zhpeer = {j: dev(zh=lax.rem(zh + j, 4)) for j in (1, 2, 3)}
    peers = [*xpeer.values(), zpeer, cpeer, zcpeer]
    if nt > 1:
        peers += [*ypeer.values(), *zhpeer.values()]
    barrier = pltpu.get_barrier_semaphore()
    for peer in peers:
        pl.semaphore_signal(barrier, inc=1, device_id=peer, device_id_type=MESH)

    n_local = 0

    def local(src, dst):
        nonlocal n_local
        copy = pltpu.make_async_copy(src, dst, ld.at[n_local])
        n_local += 1
        copy.start()
        return copy

    sent = []

    def remote(src, dst, peer):
        i = len(sent)
        copy = pltpu.make_async_remote_copy(
            src_ref=src, dst_ref=dst, send_sem=ss.at[i], recv_sem=rs.at[i], device_id=peer, device_id_type=MESH
        )
        copy.start()
        sent.append(copy)
        return copy

    small = [local(signs_hbm, signs), local(exps_hbm, exps)]
    loads = []
    for n, half in enumerate((oc, c)):
        cols = pl.ds(pl.multiple_of(half * HALF, HALF), HALF)
        loads.append([local(grads.at[pl.ds(a, 4), :, cols], g.at[n, pl.ds(a, 4)]) for a in range(0, OUTER, 4)])

    table, diagonal = inner_table()
    for copy in small:
        copy.wait()

    def sign_row(a):
        both = [signs[2 * a + i : 2 * a + i + 1, :] for i in (0, 1)]
        return (2 * jnp.concatenate(both, axis=1) - 1).astype(f32)

    def inner_pass(n):
        for a in range(OUTER):
            if a % 4 == 0:
                loads[n][a // 4].wait()
            y[a] = jnp.dot(table * sign_row(a).astype(bf16), g[n, a], preferred_element_type=f32)

    def outer_pass(k, half, dst, other=None):
        tile, part = CHUNKS[k]
        e = exps[0, 2 * half + tile]
        top = jnp.float32(0.0)
        for power in range(-4, 2):
            top = jnp.where(e == power, jnp.float32(4.0 * 2.0**power), top)
        lanes = pl.ds(tile * LANES, LANES)

        def one(i, carry):
            rows = pl.ds(pl.multiple_of(i * 32 + part * 16, 16), 16)
            values = hadamard_values([y[a, rows, lanes] for a in range(OUTER)])
            for a in range(OUTER):
                q = jnp.clip(values[a], -top, top).astype(bf16)
                at = (k, a, i // 2, i % 2)
                dst[at] = q if other is None else q + other[at]
            return carry

        lax.fori_loop(0, 8, one, 0)

    ks = range(len(CHUNKS))
    pair, a1x, a2z, a1z, a2x = {}, {}, {}, {}, {}
    inner_pass(0)
    for k in ks:
        outer_pass(k, oc, qp)
        if k == 0:
            pl.semaphore_wait(barrier, len(peers))
        pair[k] = remote(qp.at[k], pr.at[k], cpeer)
    inner_pass(1)

    for k in ks:
        pair[k].wait_recv()
        outer_pass(k, c, p, pr)
        a2z[k] = remote(p.at[k, pl.ds(NA, OUTER - NA), :, oz], rz2.at[k], zpeer)
        a1x[k] = [remote(p.at[k, pl.ds(0, NA), xo[j]], rx1.at[k, j - 1], xpeer[j]) for j in (2, 1, 3)]

    weight_load = local(weights, wv)
    for a in range(OUTER):
        signed = jnp.where(diagonal, jnp.broadcast_to(sign_row(a), (INNER, INNER)), 0.0).astype(bf16)
        hb[a] = jnp.dot(signed, table, preferred_element_type=f32).astype(bf16)

    for k in ks:
        for copy in a1x[k]:
            copy.wait_recv()

        for a in range(NA):
            total = p[k, a, x, oz].astype(f32)
            for j in range(3):
                total = total + rx1[k, j, a, oz].astype(f32)
            s1[k, a] = total.astype(bf16)
        a1z[k] = remote(s1.at[k], rz1.at[k], zpeer)
        a2z[k].wait_recv()
        for j in (2, 1, 3):
            for a in range(OUTER - NA):
                d[k, j - 1, a] = (p[k, NA + a, xo[j], z].astype(f32) + rz2[k, a, xo[j]].astype(f32)).astype(bf16)
        a2x[k] = [remote(d.at[k, j - 1], rx2.at[k, j - 1], xpeer[j]) for j in (2, 1, 3)]

    def place(k, a, x, h):
        tile, part = CHUNKS[k]
        return gv.at[2 * c + tile, a, x, h, pl.ds(part * 16, 16)]

    every, first, last = pl.ds(0, OUTER), pl.ds(0, OUTER // 2), pl.ds(OUTER // 2, OUTER // 2)
    ga, gb = pl.ds(0, NG), pl.ds(NG, OUTER - NG)
    ga_first, ga_last = pl.ds(0, NG // 2), pl.ds(NG // 2, NG - NG // 2)

    def pass_on(k, a, x, h, peer):
        return remote(place(k, a, x, h), place(k, a, x, h), peer)

    def to_core(k, x):
        tile, part = CHUNKS[k]
        block = gv.at[2 * c + tile, :, x, :, pl.ds(part * 16, 16)]
        return remote(block, block, cpeer)

    squares = jnp.zeros((16, LANES), f32)
    own_z, own_x, own_local = {}, {}, {}
    for k in ks:
        a1z[k].wait_recv()
        for copy in a2x[k]:
            copy.wait_recv()
        values = []
        for a in range(OUTER):
            total = p[k, a, x, z].astype(f32)
            if a < NA:
                for j in range(3):
                    total = total + rx1[k, j, a, z].astype(f32)
                total = total + rz1[k, a].astype(f32)
            else:
                total = total + rz2[k, a - NA, x].astype(f32)
                for j in range(3):
                    total = total + rx2[k, j, a - NA].astype(f32)
            squares = squares + total * total
            values.append(total)
        values = hadamard_values(values)
        for a in range(OUTER):
            ov[k, a] = values[a].astype(bf16)
        here = place(k, every, x, z)
        own_z[k] = remote(ov.at[k], here, zpeer)
        own_x[k] = {j: remote(ov.at[k], here, xpeer[j]) for j in (1, 3)}
        own_local[k] = local(ov.at[k], here)

    rounds = [(x, xpeer), (2 * z + c, {2: zpeer, 1: cpeer, 3: zcpeer})]
    if nt > 1:
        rounds = [(yy, ypeer), (zh, zhpeer)] + rounds
    ar_copies = []

    def ar_send(n, value):
        slot, to = rounds[n]
        ar[n, slot] = value
        ar_copies[:] = [remote(ar.at[n, slot], ar.at[n, slot], to[j]) for j in (2, 1, 3)]

    def ar_recv(n):
        for copy in ar_copies:
            copy.wait_recv()
        return (ar[n, 0] + ar[n, 1]) + (ar[n, 2] + ar[n, 3])

    ar_send(0, squares[:8] + squares[8:])
    left, right, far = xo[3], xo[1], xo[2]
    core = {k: [] for k in ks}
    relay_x, relay_z, on_x, on_x2, far_z = {}, {}, {}, {}, {}
    for k in ks:
        own_z[k].wait_recv()
        relay_x[k] = {j: pass_on(k, ga, x, oz, xpeer[j]) for j in (1, 3)}
        own_local[k].wait()
        core[k].append(to_core(k, x))
    if len(rounds) > 2:
        ar_send(1, ar_recv(0))
    for k in ks:
        own_x[k][1].wait_recv()
        on_x[k] = {1: pass_on(k, first, left, z, xpeer[1])}
        relay_z[k] = [pass_on(k, gb, left, z, zpeer)]
        own_x[k][3].wait_recv()
        on_x[k][3] = pass_on(k, last, right, z, xpeer[3])
        relay_z[k].append(pass_on(k, gb, right, z, zpeer))
    if len(rounds) > 2:
        ar_send(2, ar_recv(1))
    else:
        ar_send(1, ar_recv(0))
    for k in ks:
        relay_x[k][1].wait_recv()
        on_x2[k] = {1: pass_on(k, ga_first, left, oz, xpeer[1])}
        relay_x[k][3].wait_recv()
        on_x2[k][3] = pass_on(k, ga_last, right, oz, xpeer[3])
        on_x[k][3].wait_recv()
        far_z[k] = pass_on(k, gb, far, z, zpeer)
        relay_z[k][0].wait_recv()
        core[k].append(to_core(k, left))
        relay_z[k][1].wait_recv()
        core[k].append(to_core(k, right))
    if len(rounds) > 2:
        ar_send(3, ar_recv(2))
    for k in ks:
        on_x[k][1].wait_recv()
        on_x2[k][1].wait_recv()
        on_x2[k][3].wait_recv()
        far_z[k].wait_recv()
        core[k].append(to_core(k, far))
    total = ar_recv(len(rounds) - 1)
    total = jnp.sum(jnp.sum(total, axis=0, keepdims=True), axis=1, keepdims=True)
    factor = 0.5 / jnp.sqrt(total / (OUTER * INNER * COLS) + 1e-06)
    fac[...] = jnp.broadcast_to(factor, fac.shape)
    weight_load.wait()
    for copy in sent:
        copy.wait_send()
    for k in ks:
        for copy in core[k]:
            copy.wait_recv()


def finish(gv, wv, hb, fac, out, stage, sem):
    f32 = jnp.float32
    factor = fac[0:1, 0:1]
    copies = []
    for a in range(OUTER):
        block = jnp.concatenate([gv[i, a].reshape(INNER, LANES) for i in range(4)], axis=1)
        unrotated = jnp.dot(hb[a], block, preferred_element_type=f32)
        stage[a] = (wv[a].astype(f32) - factor * unrotated).astype(stage.dtype)
        copies.append(pltpu.make_async_copy(stage.at[a], out.at[a], sem.at[a]))
        copies[-1].start()
    for copy in copies:
        copy.wait()


def body(exponents, signs, grads, weights, nt):
    bf16, f32 = jnp.bfloat16, jnp.float32
    n_copies = 25 * len(CHUNKS) + 3 * (4 if nt > 1 else 2)
    vmem = pltpu.VMEM
    columns = grads.shape[-1]
    nk, na2 = len(CHUNKS), OUTER - NA
    chunk = (nk, OUTER, 4, 2, 16, LANES)
    any_, in_vmem = pl.BlockSpec(memory_space=pl.ANY), pl.BlockSpec(memory_space=pltpu.VMEM)
    gv, wv, hb, fac = pl.pallas_call(
        functools.partial(exchange, nt),
        out_shape=[
            vmem((4, OUTER, 4, 2, 32, LANES), bf16),
            vmem((OUTER, INNER, columns), bf16),
            vmem((OUTER, INNER, INNER), bf16),
            vmem((8, LANES), f32),
        ],
        in_specs=[any_] * 4,
        out_specs=[in_vmem] * 4,
        scratch_shapes=[
            pltpu.SMEM((1, 4), jnp.int32),
            vmem((32, LANES), jnp.int32),
            vmem((2, OUTER, INNER, HALF), bf16),
            vmem((OUTER, INNER, HALF), f32),
            vmem(chunk, bf16),
            vmem(chunk, bf16),
            vmem(chunk, bf16),
            vmem((nk, 3, NA, 2, 16, LANES), bf16),
            vmem((nk, NA, 16, LANES), bf16),
            vmem((nk, NA, 16, LANES), bf16),
            vmem((nk, na2, 4, 16, LANES), bf16),
            vmem((nk, 3, na2, 16, LANES), bf16),
            vmem((nk, 3, na2, 16, LANES), bf16),
            vmem((nk, OUTER, 16, LANES), bf16),
            vmem((4, 4, 8, LANES), f32),
            pltpu.SemaphoreType.DMA((16,)),
            pltpu.SemaphoreType.DMA((n_copies,)),
            pltpu.SemaphoreType.DMA((n_copies,)),
        ],
        compiler_params=pltpu.CompilerParams(
            collective_id=0, has_side_effects=True, vmem_limit_bytes=28 * 2**20
        ),
        name="average_step",
    )(
        pltpu.with_memory_space_constraint(exponents, pltpu.HBM),
        pltpu.with_memory_space_constraint(signs.reshape(32, LANES), pltpu.HBM),
        pltpu.with_memory_space_constraint(grads.reshape(OUTER, INNER, columns), pltpu.HBM),
        pltpu.with_memory_space_constraint(weights.reshape(OUTER, INNER, columns), pltpu.HBM),
    )
    out = pl.pallas_call(
        finish,
        out_shape=jax.ShapeDtypeStruct((OUTER, INNER, columns), bf16),
        in_specs=[in_vmem] * 4,
        out_specs=any_,
        scratch_shapes=[vmem((OUTER, INNER, columns), bf16), pltpu.SemaphoreType.DMA((OUTER,))],
        compiler_params=pltpu.CompilerParams(vmem_limit_bytes=24 * 2**20),
        name="finish_step",
    )(gv, wv, hb, fac)
    return out.reshape(OUTER * INNER, columns)


def solution(mesh):
    in_specs = (P("replica", None, "tensor"), P("replica", "tensor"), P(), P(None, "tensor"))
    nt = mesh.shape["tensor"]

    def step(grads, exponents, signs, weights):
        return body(exponents, signs, grads[0], weights, nt)

    return jax.shard_map(step, mesh=mesh, in_specs=in_specs, out_specs=P(None, "tensor"), check_vma=False)
```

```python
import functools

import jax
import jax.numpy as jnp
from jax import lax
from jax.experimental import pallas as pl
from jax.experimental.pallas import tpu as pltpu
from jax.sharding import PartitionSpec as P

COLS = 8192
OUTER, INNER = 16, 256
LANES, HALF = 128, 256
NA = 9
NG = 10
CHUNKS = [(0, 0), (0, 1), (1, 0), (1, 1)]
ORDER = [
    "vp 0", "vp 3", "vp 2", "inner 1", "vp 1", "vo 0", "sz 0", "sd 0",
    "vo 2", "sz 2", "vo 3", "vo 1", "tables 0", "sz 3", "sd 2", "a2s1 0",
    "a1s2 0", "a1s2 3", "sz 1", "a1s2 2", "sd 3", "a2s1 2", "a1z 0", "sd 1",
    "a2s2 0", "a2s1 3", "a1z 3", "a1s2 1", "a1z 2", "a2s2 2", "a2s1 1", "a2s2 3",
    "fin 0", "a1z 1", "a2s2 1", "fin 2", "fin 3", "fin 1", "sum 0", "g1 0",
    "g1 3", "gc1 3", "g2f 0", "g2f 3", "g2f 2", "g2q 3", "g1 1", "g2q 0",
    "g1 2", "g2f 1", "sum 0", "drain 0", "g2q 2", "g2q 1", "g4 0", "g3 3",
    "g3 0", "g4 3", "g4 2", "g3 1", "gc1 2", "g3 2", "g4 1", "g5 0",
    "g5 2", "g5 3", "g6 0", "gc1 1", "g5 1", "gc1 0", "g6 3", "g6 2",
    "g6 1", "sum 0",
]
MESH = pl.DeviceIdType.MESH


def hadamard_values(values):
    values = list(values)
    step = 1
    while step < len(values):
        for i in range(len(values)):
            if not i & step:
                u, v = values[i], values[i + step]
                values[i], values[i + step] = u + v, u - v
        step *= 2
    return values


def inner_table():
    row = lax.broadcasted_iota(jnp.int32, (INNER, INNER), 0)
    col = lax.broadcasted_iota(jnp.int32, (INNER, INNER), 1)
    v = row & col
    v = v ^ (v >> 4)
    v = v ^ (v >> 2)
    v = v ^ (v >> 1)
    table = (1 - 2 * (v & 1)).astype(jnp.float32) * (1.0 / 64.0)
    return table.astype(jnp.bfloat16), row == col


def exchange(
    nt, exps_hbm, signs_hbm, grads, weights,
    gv, wv, hb, fac,
    exps, signs, g, y, qp, pr, p, rt, rd, rx, t1, s1, rz1, rz2, d, ru, re, rv, t2, ov, ar, ld, ss, rs, entered,
):
    f32, bf16 = jnp.float32, jnp.bfloat16
    r, t = lax.axis_index("replica"), lax.axis_index("tensor")
    z, x, c = r // 8, (r // 2) % 4, r % 2
    zh, yy = t // 4, t % 4
    oz, oc = 1 - z, 1 - c

    def dev(z=z, x=x, c=c, zh=zh, yy=yy):
        return (z * 8 + x * 2 + c, zh * 4 + yy)

    xo = {j: lax.rem(x + j, 4) for j in (1, 2, 3)}
    xpeer = {j: dev(x=xo[j]) for j in (1, 2, 3)}
    zpeer, cpeer, zcpeer = dev(z=oz), dev(c=oc), dev(z=oz, c=oc)
    rounds = [(x, list(xpeer.values())), (2 * z + c, [zpeer, cpeer, zcpeer])]
    later = {}
    if nt > 1:
        turn = {j: (xo[j], lax.rem(yy + j, 4)) for j in (1, 2, 3)}
        turn[0] = (x, yy)
        plane = [dev(x=turn[i][0], yy=turn[j][1]) for i in range(4) for j in range(4) if i or j]
        later = {j: [] for j in (1, 2, 3)}
        for j in later:
            there = lax.rem(zh + j, 4)
            later[j] = [dev(zh=there, z=u, c=w_) for u in (z, oz) for w_ in (c, oc)]
        across = [peer for j in later for peer in later[j]]
        rounds = [(yy * 4 + x, plane), (zh * 4 + rounds[1][0], rounds[1][1] + across)]
    peers = rounds[0][1] + [zpeer, cpeer, zcpeer]
    barrier = pltpu.get_barrier_semaphore()
    for peer in peers:
        pl.semaphore_signal(barrier, inc=1, device_id=peer, device_id_type=MESH)
    for j in later:

        @pl.when(zh + j < 4)
        def greet_later(j=j):
            for peer in later[j]:
                pl.semaphore_signal(barrier, inc=1, device_id=peer, device_id_type=MESH)

    def enter():
        pl.semaphore_wait(barrier, len(peers) + (4 * zh if nt > 1 else 0))
        for j in later:

            @pl.when(zh + j >= 4)
            def answer_earlier(j=j):
                for peer in later[j]:
                    pl.semaphore_signal(entered, inc=1, device_id=peer, device_id_type=MESH)

    def await_later():
        if nt > 1:

            @pl.when(zh < 3)
            def _():
                pl.semaphore_wait(entered, 12 - 4 * zh)

    n_local = 0

    def local(src, dst):
        nonlocal n_local
        copy = pltpu.make_async_copy(src, dst, ld.at[n_local])
        n_local += 1
        copy.start()
        return copy

    sent = []

    def remote(src, dst, peer):
        i = len(sent)
        copy = pltpu.make_async_remote_copy(
            src_ref=src, dst_ref=dst, send_sem=ss.at[i], recv_sem=rs.at[i], device_id=peer, device_id_type=MESH
        )
        copy.start()
        sent.append(copy)
        return copy

    small = [local(signs_hbm, signs), local(exps_hbm, exps)]
    loads = []
    for n, half in enumerate((oc, c)):
        cols = pl.ds(pl.multiple_of(half * HALF, HALF), HALF)
        loads.append([local(grads.at[pl.ds(a, 4), :, cols], g.at[n, pl.ds(a, 4)]) for a in range(0, OUTER, 4)])

    table, diagonal = inner_table()
    for copy in small:
        copy.wait()

    def sign_row(a):
        both = [signs[2 * a + i : 2 * a + i + 1, :] for i in (0, 1)]
        return (2 * jnp.concatenate(both, axis=1) - 1).astype(f32)

    def inner_pass(n):
        for a in range(OUTER):
            if a % 4 == 0:
                loads[n][a // 4].wait()
            y[n, a] = jnp.dot(table * sign_row(a).astype(bf16), g[n, a], preferred_element_type=f32)

    def outer_pass(k, n, half, dst, other=None):
        tile, part = CHUNKS[k]
        e = exps[0, 2 * half + tile]
        top = jnp.float32(0.0)
        for power in range(-4, 2):
            top = jnp.where(e == power, jnp.float32(4.0 * 2.0**power), top)
        lanes = pl.ds(tile * LANES, LANES)

        def one(i, carry):
            rows = pl.ds(pl.multiple_of(i * 32 + part * 16, 16), 16)
            values = hadamard_values([y[n, a, rows, lanes] for a in range(OUTER)])
            for a in range(OUTER):
                q = jnp.clip(values[a], -top, top).astype(bf16)
                at = (k, a, i // 2, i % 2)
                dst[at] = q if other is None else q + other[at]
            return carry

        lax.fori_loop(0, 8, one, 0)

    inner_pass(0)
    ks = range(len(CHUNKS))
    n2 = OUTER - NA
    left, right, far = xo[3], xo[1], xo[2]
    to_right, to_left = xpeer[1], xpeer[3]
    c_ = {}
    a1 = pl.ds(0, NA)

    def split(k):
        n = (n2 + 1 - k % 2) // 2
        return n, pl.ds(0, n), pl.ds(n, n2 - n)

    def wait(k, *names):
        for name in names:
            c_[name, k].wait_recv()

    def wide(ref, *at):
        return ref[at].astype(f32)

    def other_columns(k):
        outer_pass(k, 0, oc, qp)
        if k == 0:
            enter()
        c_["pair", k] = remote(qp.at[k], pr.at[k], cpeer)

    def own_columns(k):
        wait(k, "pair")
        outer_pass(k, 1, c, p, pr)
        c_["tR", k] = remote(p.at[k, a1, far, z], rt.at[k, 0], to_right)
        c_["tL", k] = remote(p.at[k, a1, far, oz], rt.at[k, 1], to_left)

    def z_first(k):
        c_["z2", k] = remote(p.at[k, pl.ds(NA, n2), :, oz], rz2.at[k], zpeer)

    def x_direct(k):
        c_["dR", k] = remote(p.at[k, a1, right, oz], rd.at[k, 0], to_right)
        c_["dL", k] = remote(p.at[k, a1, left, z], rd.at[k, 1], to_left)

    def x_second(k):
        wait(k, "tR")
        for a in range(NA):
            t1[k, 0, a] = rt[k, 0, a] + p[k, a, right, z]
        c_["xR", k] = remote(t1.at[k, 0], rx.at[k, 0], to_right)
        wait(k, "tL")
        for a in range(NA):
            t1[k, 1, a] = rt[k, 1, a] + p[k, a, left, oz]
        c_["xL", k] = remote(t1.at[k, 1], rx.at[k, 1], to_left)

    def z_then_x(k):
        wait(k, "z2")
        n, upper, lower = split(k)
        for j in (2, 1, 3):
            for a in range(n2):
                d[k, j - 1, a] = p[k, NA + a, xo[j], z] + rz2[k, a, xo[j]]
            if j == 2:
                c_["uR", k] = remote(d.at[k, 1, upper], ru.at[k, upper], to_right)
                c_["uL", k] = remote(d.at[k, 1, lower], ru.at[k, lower], to_left)
        c_["eR", k] = remote(d.at[k, 0, lower], re.at[k, lower], to_right)
        c_["eL", k] = remote(d.at[k, 2, upper], re.at[k, upper], to_left)

    def x_then_z(k):
        wait(k, "dR", "xL")
        for a in range(NA):
            s1[k, a] = (wide(p, k, a, x, oz) + wide(rd, k, 0, a) + wide(rx, k, 1, a)).astype(bf16)
        c_["z1", k] = remote(s1.at[k], rz1.at[k], zpeer)

    def x_second_after_z(k):
        n, upper, lower = split(k)
        wait(k, "uR")
        for a in range(n):
            t2[k, a] = ru[k, a] + d[k, 0, a]
        c_["vR", k] = remote(t2.at[k, upper], rv.at[k, upper], to_right)
        wait(k, "uL")
        for a in range(n, n2):
            t2[k, a] = ru[k, a] + d[k, 2, a]
        c_["vL", k] = remote(t2.at[k, lower], rv.at[k, lower], to_left)

    def place(k, a, x, h):
        tile, part = CHUNKS[k]
        return gv.at[2 * c + tile, a, x, h, pl.ds(part * 16, 16)]

    every, first, last = pl.ds(0, OUTER), pl.ds(0, OUTER // 2), pl.ds(OUTER // 2, OUTER // 2)
    ga, gb = pl.ds(0, NG), pl.ds(NG, OUTER - NG)
    ga_first, ga_last = pl.ds(0, NG // 2), pl.ds(NG // 2, NG - NG // 2)

    def pass_on(name, k, a, x, h, peer):
        c_[name, k] = remote(place(k, a, x, h), place(k, a, x, h), peer)

    def to_core(name, k, x):
        tile, part = CHUNKS[k]
        block = gv.at[2 * c + tile, :, x, :, pl.ds(part * 16, 16)]
        c_[name, k] = remote(block, block, cpeer)

    squares = []

    def own_rows(k):
        wait(k, "dL", "xR", "eR", "eL", "vR", "vL", "z1")
        values, square = [], jnp.zeros((16, LANES), f32)
        for a in range(OUTER):
            total = wide(p, k, a, x, z)
            if a < NA:
                total = total + wide(rd, k, 1, a) + wide(rx, k, 0, a) + wide(rz1, k, a)
            else:
                total = total + wide(rz2, k, a - NA, x) + wide(re, k, a - NA) + wide(rv, k, a - NA)
            square = square + total * total
            values.append(total)
        squares.append(square)
        values = hadamard_values(values)
        for a in range(OUTER):
            ov[k, a] = values[a].astype(bf16)
        here = place(k, every, x, z)
        c_["oz", k] = remote(ov.at[k], here, zpeer)
        c_["oR", k] = remote(ov.at[k], here, to_right)
        c_["oL", k] = remote(ov.at[k], here, to_left)
        c_["own", k] = local(ov.at[k], here)

    def gather_z(k):
        wait(k, "oz")
        pass_on("rR", k, ga, x, oz, to_right)
        pass_on("rL", k, ga, x, oz, to_left)

    def core_own(k):
        c_["own", k].wait()
        to_core("c1", k, x)

    def gather_x(k):
        wait(k, "oR")
        pass_on("fR", k, first, left, z, to_right)
        wait(k, "oL")
        pass_on("fL", k, last, right, z, to_left)

    def gather_x_z(k):
        pass_on("qa", k, gb, left, z, zpeer)
        pass_on("qb", k, gb, right, z, zpeer)

    def gather_x_second(k):
        wait(k, "rR")
        pass_on("hR", k, ga_first, left, oz, to_right)
        wait(k, "rL")
        pass_on("hL", k, ga_last, right, oz, to_left)

    def gather_far_z(k):
        wait(k, "fL")
        pass_on("qc", k, gb, far, z, zpeer)

    def core_near(k):
        wait(k, "qa")
        to_core("c2", k, left)
        wait(k, "qb")
        to_core("c3", k, right)

    def core_far(k):
        wait(k, "fR", "hR", "hL", "qc")
        to_core("c4", k, far)

    ar_copies = []
    ar_round = 0

    def sum_round():
        nonlocal ar_round
        n = ar_round
        ar_round += 1
        if n == 0:
            total = functools.reduce(lambda u, v: u + v, squares)
            total = total[:8] + total[8:]
        else:
            for copy in ar_copies:
                copy.wait_recv()
            slots = len(rounds[n - 1][1]) + 1
            total = functools.reduce(lambda u, v: u + v, [ar[n - 1, i] for i in range(slots)])
        if n == len(rounds):
            return total
        slot, to = rounds[n]
        ar[n, slot] = total
        if n == 1:
            await_later()
        ar_copies[:] = [remote(ar.at[n, slot], ar.at[n, slot], peer) for peer in to]
        return None

    drained = 0

    def drain(upto):
        nonlocal drained
        for copy in sent[drained:upto]:
            copy.wait_send()
        drained = upto

    steps = dict(
        vp=other_columns,
        vo=own_columns,
        sd=x_direct,
        sz=z_first,
        a1s2=x_second,
        a2s1=z_then_x,
        a1z=x_then_z,
        a2s2=x_second_after_z,
        fin=own_rows,
        g1=gather_z,
        gc1=core_own,
        g2f=gather_x,
        g2q=gather_x_z,
        g3=gather_x_second,
        g4=gather_far_z,
        g5=core_near,
        g6=core_far,
    )
    total, weight_load, scattered = None, None, 0
    for step in ORDER:
        name, k = step.split()
        if name == "inner":
            inner_pass(1)
        elif name == "tables":
            weight_load = local(weights, wv)
            for a in range(OUTER):
                signed = jnp.where(diagonal, jnp.broadcast_to(sign_row(a), (INNER, INNER)), 0.0).astype(bf16)
                hb[a] = jnp.dot(signed, table, preferred_element_type=f32).astype(bf16)
        elif name == "sum":
            scattered = scattered or len(sent)
            got = sum_round()
            total = total if got is None else got
        elif name == "drain":
            drain(scattered)
        else:
            steps[name](int(k))

    total = jnp.sum(jnp.sum(total, axis=0, keepdims=True), axis=1, keepdims=True)
    factor = 0.5 / jnp.sqrt(total / (OUTER * INNER * COLS) + 1e-06)
    fac[...] = jnp.broadcast_to(factor, fac.shape)
    weight_load.wait()
    drain(len(sent))
    for k in ks:
        wait(k, "c1", "c2", "c3", "c4")


def finish(gv, wv, hb, fac, out, stage, sem):
    f32 = jnp.float32
    factor = fac[0:1, 0:1]
    copies = []
    for a in range(OUTER):
        block = jnp.concatenate([gv[i, a].reshape(INNER, LANES) for i in range(4)], axis=1)
        unrotated = jnp.dot(hb[a], block, preferred_element_type=f32)
        stage[a] = (wv[a].astype(f32) - factor * unrotated).astype(stage.dtype)
        copies.append(pltpu.make_async_copy(stage.at[a], out.at[a], sem.at[a]))
        copies[-1].start()
    for copy in copies:
        copy.wait()


def body(exponents, signs, grads, weights, nt):
    bf16, f32 = jnp.bfloat16, jnp.float32
    n_copies = 31 * len(CHUNKS) + 2 * (15 if nt > 1 else 3)
    vmem = pltpu.VMEM
    columns = grads.shape[-1]
    nk, na2 = len(CHUNKS), OUTER - NA
    chunk = (nk, OUTER, 4, 2, 16, LANES)
    any_, in_vmem = pl.BlockSpec(memory_space=pl.ANY), pl.BlockSpec(memory_space=pltpu.VMEM)
    gv, wv, hb, fac = pl.pallas_call(
        functools.partial(exchange, nt),
        out_shape=[
            vmem((4, OUTER, 4, 2, 32, LANES), bf16),
            vmem((OUTER, INNER, columns), bf16),
            vmem((OUTER, INNER, INNER), bf16),
            vmem((8, LANES), f32),
        ],
        in_specs=[any_] * 4,
        out_specs=[in_vmem] * 4,
        scratch_shapes=[
            pltpu.SMEM((1, 4), jnp.int32),
            vmem((32, LANES), jnp.int32),
            vmem((2, OUTER, INNER, HALF), bf16),
            vmem((2, OUTER, INNER, HALF), f32),
            vmem(chunk, bf16),
            vmem(chunk, bf16),
            vmem(chunk, bf16),
            vmem((nk, 2, NA, 16, LANES), bf16),
            vmem((nk, 2, NA, 16, LANES), bf16),
            vmem((nk, 2, NA, 16, LANES), bf16),
            vmem((nk, 2, NA, 16, LANES), bf16),
            vmem((nk, NA, 16, LANES), bf16),
            vmem((nk, NA, 16, LANES), bf16),
            vmem((nk, na2, 4, 16, LANES), bf16),
            vmem((nk, 3, na2, 16, LANES), bf16),
            vmem((nk, na2, 16, LANES), bf16),
            vmem((nk, na2, 16, LANES), bf16),
            vmem((nk, na2, 16, LANES), bf16),
            vmem((nk, na2, 16, LANES), bf16),
            vmem((nk, OUTER, 16, LANES), bf16),
            vmem((2, 16, 8, LANES), f32),
            pltpu.SemaphoreType.DMA((16,)),
            pltpu.SemaphoreType.DMA((n_copies,)),
            pltpu.SemaphoreType.DMA((n_copies,)),
            pltpu.SemaphoreType.REGULAR,
        ],
        compiler_params=pltpu.CompilerParams(
            collective_id=0, has_side_effects=True, vmem_limit_bytes=30 * 2**20
        ),
        name="average_step",
    )(
        pltpu.with_memory_space_constraint(exponents, pltpu.HBM),
        pltpu.with_memory_space_constraint(signs.reshape(32, LANES), pltpu.HBM),
        pltpu.with_memory_space_constraint(grads.reshape(OUTER, INNER, columns), pltpu.HBM),
        pltpu.with_memory_space_constraint(weights.reshape(OUTER, INNER, columns), pltpu.HBM),
    )
    out = pl.pallas_call(
        finish,
        out_shape=jax.ShapeDtypeStruct((OUTER, INNER, columns), bf16),
        in_specs=[in_vmem] * 4,
        out_specs=any_,
        scratch_shapes=[vmem((OUTER, INNER, columns), bf16), pltpu.SemaphoreType.DMA((OUTER,))],
        compiler_params=pltpu.CompilerParams(vmem_limit_bytes=24 * 2**20),
        name="finish_step",
    )(gv, wv, hb, fac)
    return out.reshape(OUTER * INNER, columns)


def solution(mesh):
    in_specs = (P("replica", None, "tensor"), P("replica", "tensor"), P(), P(None, "tensor"))
    nt = mesh.shape["tensor"]

    def step(grads, exponents, signs, weights):
        return body(exponents, signs, grads[0], weights, nt)

    return jax.shard_map(step, mesh=mesh, in_specs=in_specs, out_specs=P(None, "tensor"), check_vma=False)
```

```python
import functools

import jax
import jax.numpy as jnp
from jax import lax
from jax.experimental import pallas as pl
from jax.experimental.pallas import tpu as pltpu
from jax.sharding import PartitionSpec as P

COLS = 8192
OUTER, INNER = 16, 256
LANES, HALF = 128, 256
NA = 9
NG = 10
CHUNKS = [(0, 0), (0, 1), (1, 0), (1, 1)]
ORDER = [
    "vp 0", "vp 3", "vp 2", "inner 1", "vp 1", "vo 0", "sz 0", "sd 0",
    "vo 2", "sz 2", "vo 3", "vo 1", "tables 0", "sz 3", "sd 2", "a2s1 0",
    "a1s2 0", "a1s2 3", "sz 1", "a1s2 2", "sd 3", "a2s1 2", "a1z 0", "sd 1",
    "a2s2 0", "a2s1 3", "a1z 3", "a1s2 1", "a1z 2", "a2s2 2", "a2s1 1", "a2s2 3",
    "fin 0", "a1z 1", "a2s2 1", "fin 2", "fin 3", "drain 0", "fin 1", "sum 0",
    "g1 0", "g1 3", "gc1 3", "g2f 0", "g2f 3", "g2f 2", "g2q 3", "g1 1",
    "g2q 0", "g1 2", "g2f 1", "sum 0", "g2q 2", "g2q 1", "g4 0", "g3 3",
    "g3 0", "g4 3", "drain 0", "g4 2", "g3 1", "gc1 2", "g3 2", "g4 1",
    "g5 0", "g5 2", "g5 3", "drain 0", "g6 0", "gc1 1", "g5 1", "gc1 0",
    "g6 3", "g6 2", "drain 0", "g6 1", "sum 0",
]
MESH = pl.DeviceIdType.MESH


def hadamard_values(values):
    values = list(values)
    step = 1
    while step < len(values):
        for i in range(len(values)):
            if not i & step:
                u, v = values[i], values[i + step]
                values[i], values[i + step] = u + v, u - v
        step *= 2
    return values


def inner_table():
    row = lax.broadcasted_iota(jnp.int32, (INNER, INNER), 0)
    col = lax.broadcasted_iota(jnp.int32, (INNER, INNER), 1)
    v = row & col
    v = v ^ (v >> 4)
    v = v ^ (v >> 2)
    v = v ^ (v >> 1)
    table = (1 - 2 * (v & 1)).astype(jnp.float32) * (1.0 / 64.0)
    return table.astype(jnp.bfloat16), row == col


def exchange(
    nt, exps_hbm, signs_hbm, grads, weights,
    gv, wv, hb, fac,
    exps, signs, g, y, qp, pr, p, rt, rd, rx, t1, s1, rz1, rz2, d, ru, re, rv, t2, ov, ar, ld, ss, rs, entered,
):
    f32, bf16 = jnp.float32, jnp.bfloat16
    r, t = lax.axis_index("replica"), lax.axis_index("tensor")
    z, x, c = r // 8, (r // 2) % 4, r % 2
    zh, yy = t // 4, t % 4
    oz, oc = 1 - z, 1 - c

    def dev(z=z, x=x, c=c, zh=zh, yy=yy):
        return (z * 8 + x * 2 + c, zh * 4 + yy)

    xo = {j: lax.rem(x + j, 4) for j in (1, 2, 3)}
    xpeer = {j: dev(x=xo[j]) for j in (1, 2, 3)}
    zpeer, cpeer, zcpeer = dev(z=oz), dev(c=oc), dev(z=oz, c=oc)
    rounds = [(x, list(xpeer.values())), (2 * z + c, [zpeer, cpeer, zcpeer])]
    later = {}
    if nt > 1:
        turn = {j: (xo[j], lax.rem(yy + j, 4)) for j in (1, 2, 3)}
        turn[0] = (x, yy)
        plane = [dev(x=turn[i][0], yy=turn[j][1]) for i in range(4) for j in range(4) if i or j]
        later = {j: [] for j in (1, 2, 3)}
        for j in later:
            there = lax.rem(zh + j, 4)
            later[j] = [dev(zh=there, z=u, c=w_) for u in (z, oz) for w_ in (c, oc)]
        across = [peer for j in later for peer in later[j]]
        rounds = [(yy * 4 + x, plane), (zh * 4 + rounds[1][0], rounds[1][1] + across)]
    n_local = 0

    def local(src, dst):
        nonlocal n_local
        copy = pltpu.make_async_copy(src, dst, ld.at[n_local])
        n_local += 1
        copy.start()
        return copy

    loads = []
    for n, half in enumerate((oc, c)):
        cols = pl.ds(pl.multiple_of(half * HALF, HALF), HALF)
        loads.append([local(grads.at[pl.ds(a, 4), :, cols], g.at[n, pl.ds(a, 4)]) for a in range(0, OUTER, 4)])
        if n == 0:
            small = [local(signs_hbm, signs), local(exps_hbm, exps)]

    peers = rounds[0][1] + [zpeer, cpeer, zcpeer]
    barrier = pltpu.get_barrier_semaphore()
    for peer in peers:
        pl.semaphore_signal(barrier, inc=1, device_id=peer, device_id_type=MESH)
    for j in later:

        @pl.when(zh + j < 4)
        def greet_later(j=j):
            for peer in later[j]:
                pl.semaphore_signal(barrier, inc=1, device_id=peer, device_id_type=MESH)

    def enter():
        pl.semaphore_wait(barrier, len(peers) + (4 * zh if nt > 1 else 0))
        for j in later:

            @pl.when(zh + j >= 4)
            def answer_earlier(j=j):
                for peer in later[j]:
                    pl.semaphore_signal(entered, inc=1, device_id=peer, device_id_type=MESH)

    def await_later():
        if nt > 1:

            @pl.when(zh < 3)
            def _():
                pl.semaphore_wait(entered, 12 - 4 * zh)

    sent = []

    def remote(src, dst, peer):
        i = len(sent)
        copy = pltpu.make_async_remote_copy(
            src_ref=src, dst_ref=dst, send_sem=ss.at[i], recv_sem=rs.at[i], device_id=peer, device_id_type=MESH
        )
        copy.start()
        sent.append(copy)
        return copy

    table, diagonal = inner_table()
    for copy in small:
        copy.wait()

    def sign_row(a):
        both = [signs[2 * a + i : 2 * a + i + 1, :] for i in (0, 1)]
        return (2 * jnp.concatenate(both, axis=1) - 1).astype(f32)

    def inner_pass(n):
        for a in range(OUTER):
            if a % 4 == 0:
                loads[n][a // 4].wait()
            y[n, a] = jnp.dot(table * sign_row(a).astype(bf16), g[n, a], preferred_element_type=f32)

    def outer_pass(k, n, half, dst, other=None):
        tile, part = CHUNKS[k]
        e = exps[0, 2 * half + tile]
        top = jnp.float32(0.0)
        for power in range(-4, 2):
            top = jnp.where(e == power, jnp.float32(4.0 * 2.0**power), top)
        lanes = pl.ds(tile * LANES, LANES)

        def one(i, carry):
            rows = pl.ds(pl.multiple_of(i * 32 + part * 16, 16), 16)
            values = hadamard_values([y[n, a, rows, lanes] for a in range(OUTER)])
            for a in range(OUTER):
                q = jnp.clip(values[a], -top, top).astype(bf16)
                at = (k, a, i // 2, i % 2)
                dst[at] = q if other is None else q + other[at]
            return carry

        lax.fori_loop(0, 8, one, 0)

    inner_pass(0)
    ks = range(len(CHUNKS))
    n2 = OUTER - NA
    left, right, far = xo[3], xo[1], xo[2]
    to_right, to_left = xpeer[1], xpeer[3]
    c_ = {}
    a1 = pl.ds(0, NA)

    def split(k):
        n = (n2 + 1 - k % 2) // 2
        return n, pl.ds(0, n), pl.ds(n, n2 - n)

    def wait(k, *names):
        for name in names:
            c_[name, k].wait_recv()

    def wide(ref, *at):
        return ref[at].astype(f32)

    def other_columns(k):
        outer_pass(k, 0, oc, qp)
        if k == 0:
            enter()
        c_["pair", k] = remote(qp.at[k], pr.at[k], cpeer)

    def own_columns(k):
        wait(k, "pair")
        outer_pass(k, 1, c, p, pr)
        c_["tR", k] = remote(p.at[k, a1, far, z], rt.at[k, 0], to_right)
        c_["tL", k] = remote(p.at[k, a1, far, oz], rt.at[k, 1], to_left)

    def z_first(k):
        c_["z2", k] = remote(p.at[k, pl.ds(NA, n2), :, oz], rz2.at[k], zpeer)

    def x_direct(k):
        c_["dR", k] = remote(p.at[k, a1, right, oz], rd.at[k, 0], to_right)
        c_["dL", k] = remote(p.at[k, a1, left, z], rd.at[k, 1], to_left)

    def x_second(k):
        wait(k, "tR")
        for a in range(NA):
            t1[k, 0, a] = rt[k, 0, a] + p[k, a, right, z]
        c_["xR", k] = remote(t1.at[k, 0], rx.at[k, 0], to_right)
        wait(k, "tL")
        for a in range(NA):
            t1[k, 1, a] = rt[k, 1, a] + p[k, a, left, oz]
        c_["xL", k] = remote(t1.at[k, 1], rx.at[k, 1], to_left)

    def z_then_x(k):
        wait(k, "z2")
        n, upper, lower = split(k)
        for j in (2, 1, 3):
            for a in range(n2):
                d[k, j - 1, a] = p[k, NA + a, xo[j], z] + rz2[k, a, xo[j]]
            if j == 2:
                c_["uR", k] = remote(d.at[k, 1, upper], ru.at[k, upper], to_right)
                c_["uL", k] = remote(d.at[k, 1, lower], ru.at[k, lower], to_left)
        c_["eR", k] = remote(d.at[k, 0, lower], re.at[k, lower], to_right)
        c_["eL", k] = remote(d.at[k, 2, upper], re.at[k, upper], to_left)

    def x_then_z(k):
        wait(k, "dR", "xL")
        for a in range(NA):
            s1[k, a] = (wide(p, k, a, x, oz) + wide(rd, k, 0, a) + wide(rx, k, 1, a)).astype(bf16)
        c_["z1", k] = remote(s1.at[k], rz1.at[k], zpeer)

    def x_second_after_z(k):
        n, upper, lower = split(k)
        wait(k, "uR")
        for a in range(n):
            t2[k, a] = ru[k, a] + d[k, 0, a]
        c_["vR", k] = remote(t2.at[k, upper], rv.at[k, upper], to_right)
        wait(k, "uL")
        for a in range(n, n2):
            t2[k, a] = ru[k, a] + d[k, 2, a]
        c_["vL", k] = remote(t2.at[k, lower], rv.at[k, lower], to_left)

    def place(k, a, x, h):
        tile, part = CHUNKS[k]
        return gv.at[2 * c + tile, a, x, h, pl.ds(part * 16, 16)]

    every, first, last = pl.ds(0, OUTER), pl.ds(0, OUTER // 2), pl.ds(OUTER // 2, OUTER // 2)
    ga, gb = pl.ds(0, NG), pl.ds(NG, OUTER - NG)
    ga_first, ga_last = pl.ds(0, NG // 2), pl.ds(NG // 2, NG - NG // 2)

    def pass_on(name, k, a, x, h, peer):
        c_[name, k] = remote(place(k, a, x, h), place(k, a, x, h), peer)

    def to_core(name, k, x):
        tile, part = CHUNKS[k]
        block = gv.at[2 * c + tile, :, x, :, pl.ds(part * 16, 16)]
        c_[name, k] = remote(block, block, cpeer)

    squares = []

    def own_rows(k):
        wait(k, "dL", "xR", "eR", "eL", "vR", "vL", "z1")
        values, square = [], jnp.zeros((16, LANES), f32)
        for a in range(OUTER):
            total = wide(p, k, a, x, z)
            if a < NA:
                total = total + wide(rd, k, 1, a) + wide(rx, k, 0, a) + wide(rz1, k, a)
            else:
                total = total + wide(rz2, k, a - NA, x) + wide(re, k, a - NA) + wide(rv, k, a - NA)
            square = square + total * total
            values.append(total)
        squares.append(square)
        values = hadamard_values(values)
        for a in range(OUTER):
            ov[k, a] = values[a].astype(bf16)
        here = place(k, every, x, z)
        c_["oz", k] = remote(ov.at[k], here, zpeer)
        c_["oR", k] = remote(ov.at[k], here, to_right)
        c_["oL", k] = remote(ov.at[k], here, to_left)
        c_["own", k] = local(ov.at[k], here)

    def gather_z(k):
        wait(k, "oz")
        pass_on("rR", k, ga, x, oz, to_right)
        pass_on("rL", k, ga, x, oz, to_left)

    def core_own(k):
        c_["own", k].wait()
        to_core("c1", k, x)

    def gather_x(k):
        wait(k, "oR")
        pass_on("fR", k, first, left, z, to_right)
        wait(k, "oL")
        pass_on("fL", k, last, right, z, to_left)

    def gather_x_z(k):
        pass_on("qa", k, gb, left, z, zpeer)
        pass_on("qb", k, gb, right, z, zpeer)

    def gather_x_second(k):
        wait(k, "rR")
        pass_on("hR", k, ga_first, left, oz, to_right)
        wait(k, "rL")
        pass_on("hL", k, ga_last, right, oz, to_left)

    def gather_far_z(k):
        wait(k, "fL")
        pass_on("qc", k, gb, far, z, zpeer)

    def core_near(k):
        wait(k, "qa")
        to_core("c2", k, left)
        wait(k, "qb")
        to_core("c3", k, right)

    def core_far(k):
        wait(k, "fR", "hR", "hL", "qc")
        to_core("c4", k, far)

    ar_copies = []
    ar_round = 0

    def sum_round():
        nonlocal ar_round
        n = ar_round
        ar_round += 1
        if n == 0:
            total = functools.reduce(lambda u, v: u + v, squares)
            total = jnp.sum(total, axis=0, keepdims=True)
        else:
            for copy in ar_copies:
                copy.wait_recv()
            slots = len(rounds[n - 1][1]) + 1
            total = functools.reduce(lambda u, v: u + v, [ar[n - 1, i] for i in range(slots)])
        if n == len(rounds):
            return total
        slot, to = rounds[n]
        ar[n, slot] = total
        if n == 1:
            await_later()
        ar_copies[:] = [remote(ar.at[n, slot], ar.at[n, slot], peer) for peer in to]
        return None

    drained = 0

    def drain(upto):
        nonlocal drained
        for copy in sent[drained:upto]:
            copy.wait_send()
        drained = upto

    steps = dict(
        vp=other_columns,
        vo=own_columns,
        sd=x_direct,
        sz=z_first,
        a1s2=x_second,
        a2s1=z_then_x,
        a1z=x_then_z,
        a2s2=x_second_after_z,
        fin=own_rows,
        g1=gather_z,
        gc1=core_own,
        g2f=gather_x,
        g2q=gather_x_z,
        g3=gather_x_second,
        g4=gather_far_z,
        g5=core_near,
        g6=core_far,
    )
    total, weight_load, mark = None, None, 0
    for step in ORDER:
        name, k = step.split()
        if name == "inner":
            inner_pass(1)
        elif name == "tables":
            weight_load = local(weights, wv)
            for a in range(OUTER):
                signed = jnp.where(diagonal, jnp.broadcast_to(sign_row(a), (INNER, INNER)), 0.0).astype(bf16)
                hb[a] = jnp.dot(signed, table, preferred_element_type=f32).astype(bf16)
        elif name == "sum":
            got = sum_round()
            total = total if got is None else got
        elif name == "drain":
            drain(mark)
            mark = len(sent)
        else:
            steps[name](int(k))

    total = jnp.sum(total, axis=1, keepdims=True)
    factor = 0.5 / jnp.sqrt(total / (OUTER * INNER * COLS) + 1e-06)
    fac[...] = jnp.broadcast_to(factor, fac.shape)
    weight_load.wait()
    drain(len(sent))
    for k in ks:
        wait(k, "c1", "c2", "c3", "c4")


def finish(gv, wv, hb, fac, out, stage, sem):
    f32 = jnp.float32
    factor = fac[0:1, 0:1]
    copies = []
    for a in range(OUTER):
        block = jnp.concatenate([gv[i, a].reshape(INNER, LANES) for i in range(4)], axis=1)
        unrotated = jnp.dot(hb[a], block, preferred_element_type=f32)
        stage[a] = (wv[a].astype(f32) - factor * unrotated).astype(stage.dtype)
        copies.append(pltpu.make_async_copy(stage.at[a], out.at[a], sem.at[a]))
        copies[-1].start()
    for copy in copies:
        copy.wait()


def body(exponents, signs, grads, weights, nt):
    bf16, f32 = jnp.bfloat16, jnp.float32
    n_copies = 31 * len(CHUNKS) + 2 * (15 if nt > 1 else 3)
    vmem = pltpu.VMEM
    columns = grads.shape[-1]
    nk, na2 = len(CHUNKS), OUTER - NA
    chunk = (nk, OUTER, 4, 2, 16, LANES)
    any_, in_vmem = pl.BlockSpec(memory_space=pl.ANY), pl.BlockSpec(memory_space=pltpu.VMEM)
    gv, wv, hb, fac = pl.pallas_call(
        functools.partial(exchange, nt),
        out_shape=[
            vmem((4, OUTER, 4, 2, 32, LANES), bf16),
            vmem((OUTER, INNER, columns), bf16),
            vmem((OUTER, INNER, INNER), bf16),
            vmem((8, LANES), f32),
        ],
        in_specs=[any_] * 4,
        out_specs=[in_vmem] * 4,
        scratch_shapes=[
            pltpu.SMEM((1, 4), jnp.int32),
            vmem((32, LANES), jnp.int32),
            vmem((2, OUTER, INNER, HALF), bf16),
            vmem((2, OUTER, INNER, HALF), f32),
            vmem(chunk, bf16),
            vmem(chunk, bf16),
            vmem(chunk, bf16),
            vmem((nk, 2, NA, 16, LANES), bf16),
            vmem((nk, 2, NA, 16, LANES), bf16),
            vmem((nk, 2, NA, 16, LANES), bf16),
            vmem((nk, 2, NA, 16, LANES), bf16),
            vmem((nk, NA, 16, LANES), bf16),
            vmem((nk, NA, 16, LANES), bf16),
            vmem((nk, na2, 4, 16, LANES), bf16),
            vmem((nk, 3, na2, 16, LANES), bf16),
            vmem((nk, na2, 16, LANES), bf16),
            vmem((nk, na2, 16, LANES), bf16),
            vmem((nk, na2, 16, LANES), bf16),
            vmem((nk, na2, 16, LANES), bf16),
            vmem((nk, OUTER, 16, LANES), bf16),
            vmem((2, 16, 1, LANES), f32),
            pltpu.SemaphoreType.DMA((16,)),
            pltpu.SemaphoreType.DMA((n_copies,)),
            pltpu.SemaphoreType.DMA((n_copies,)),
            pltpu.SemaphoreType.REGULAR,
        ],
        compiler_params=pltpu.CompilerParams(
            collective_id=0, has_side_effects=True, vmem_limit_bytes=30 * 2**20
        ),
        name="average_step",
    )(
        pltpu.with_memory_space_constraint(exponents, pltpu.HBM),
        pltpu.with_memory_space_constraint(signs.reshape(32, LANES), pltpu.HBM),
        pltpu.with_memory_space_constraint(grads.reshape(OUTER, INNER, columns), pltpu.HBM),
        pltpu.with_memory_space_constraint(weights.reshape(OUTER, INNER, columns), pltpu.HBM),
    )
    out = pl.pallas_call(
        finish,
        out_shape=jax.ShapeDtypeStruct((OUTER, INNER, columns), bf16),
        in_specs=[in_vmem] * 4,
        out_specs=any_,
        scratch_shapes=[vmem((OUTER, INNER, columns), bf16), pltpu.SemaphoreType.DMA((OUTER,))],
        compiler_params=pltpu.CompilerParams(vmem_limit_bytes=24 * 2**20),
        name="finish_step",
    )(gv, wv, hb, fac)
    return out.reshape(OUTER * INNER, columns)


def solution(mesh):
    in_specs = (P("replica", None, "tensor"), P("replica", "tensor"), P(), P(None, "tensor"))
    nt = mesh.shape["tensor"]

    def step(grads, exponents, signs, weights):
        return body(exponents, signs, grads[0], weights, nt)

    return jax.shard_map(step, mesh=mesh, in_specs=in_specs, out_specs=P(None, "tensor"), check_vma=False)
```

```python
import functools

import jax
import jax.numpy as jnp
from jax import lax
from jax.experimental import pallas as pl
from jax.experimental.pallas import tpu as pltpu
from jax.sharding import PartitionSpec as P

COLS = 8192
OUTER, INNER = 16, 256
LANES, HALF = 128, 256
NA = 9
NG = 10
CHUNKS = [(0, 0), (0, 1), (1, 0), (1, 1)]
ORDER = [
    "vp 0", "inner 1", "vp 2", "vp 1", "vo 0", "sz 0", "sd 0", "vp 3",
    "vo 2", "vo 1", "sd 1", "sz 1", "vo 3", "a1s2 0", "sz 3", "sz 2",
    "sd 2", "a1s2 1", "a2s1 0", "a1s2 3", "sd 3", "a1z 0", "a2s1 1", "a1s2 2",
    "a2s1 3", "a1z 1", "a2s2 0", "a2s1 2", "a1z 3", "a2s2 1", "a1z 2", "a2s2 3",
    "fin 0", "a2s2 2", "fin 1", "fin 3", "g1 0", "drain 0", "fin 2", "sum 0",
    "g2f 0", "g1 3", "g2f 3", "g1 1", "g2q 0", "g2q 3", "g1 2", "g2f 2",
    "g2f 1", "g3 0", "g2q 1", "sum 0", "g4 0", "g2q 2", "g5 0", "gc1 1",
    "gc1 3", "g3 1", "g4 3", "gc1 0", "g3 3", "drain 0", "g3 2", "g4 2",
    "gc1 2", "g5 1", "g4 1", "tables 0", "g5 3", "g5 2", "drain 0", "g6 3",
    "g6 0", "g6 2", "drain 0", "g6 1", "sum 0",
]
MESH = pl.DeviceIdType.MESH


def hadamard_values(values):
    values = list(values)
    step = 1
    while step < len(values):
        for i in range(len(values)):
            if not i & step:
                u, v = values[i], values[i + step]
                values[i], values[i + step] = u + v, u - v
        step *= 2
    return values


def inner_table():
    row = lax.broadcasted_iota(jnp.int32, (INNER, INNER), 0)
    col = lax.broadcasted_iota(jnp.int32, (INNER, INNER), 1)
    v = row & col
    v = v ^ (v >> 4)
    v = v ^ (v >> 2)
    v = v ^ (v >> 1)
    table = (1 - 2 * (v & 1)).astype(jnp.float32) * (1.0 / 64.0)
    return table.astype(jnp.bfloat16), row == col


def exchange(
    nt, exps_hbm, signs_hbm, grads, weights,
    gv, wv, hb, fac,
    exps, signs, g, y, qp, pr, p, rt, rd, rx, t1, s1, rz1, rz2, d, ru, re, rv, t2, ov, ar, ld, ss, rs, entered,
):
    f32, bf16 = jnp.float32, jnp.bfloat16
    r, t = lax.axis_index("replica"), lax.axis_index("tensor")
    z, x, c = r // 8, (r // 2) % 4, r % 2
    zh, yy = t // 4, t % 4
    oz, oc = 1 - z, 1 - c

    def dev(z=z, x=x, c=c, zh=zh, yy=yy):
        return (z * 8 + x * 2 + c, zh * 4 + yy)

    xo = {j: lax.rem(x + j, 4) for j in (1, 2, 3)}
    xpeer = {j: dev(x=xo[j]) for j in (1, 2, 3)}
    zpeer, cpeer, zcpeer = dev(z=oz), dev(c=oc), dev(z=oz, c=oc)
    rounds = [(x, list(xpeer.values())), (2 * z + c, [zpeer, cpeer, zcpeer])]
    later, later_y = {}, {}
    if nt > 1:
        turn = {j: (xo[j], lax.rem(yy + j, 4)) for j in (1, 2, 3)}
        turn[0] = (x, yy)
        plane = [dev(x=turn[i][0], yy=turn[j][1]) for i in range(4) for j in range(4) if i or j]
        later_y = {j: [dev(x=turn[i][0], yy=turn[j][1]) for i in range(4)] for j in (1, 2, 3)}
        later = {j: [] for j in (1, 2, 3)}
        for j in later:
            there = lax.rem(zh + j, 4)
            later[j] = [dev(zh=there, z=u, c=w_) for u in (z, oz) for w_ in (c, oc)]
        across = [peer for j in later for peer in later[j]]
        rounds = [(yy * 4 + x, plane), (zh * 4 + rounds[1][0], rounds[1][1] + across)]
    n_local = 0

    def local(src, dst):
        nonlocal n_local
        copy = pltpu.make_async_copy(src, dst, ld.at[n_local])
        n_local += 1
        copy.start()
        return copy

    loads = []
    for n, half in enumerate((oc, c)):
        cols = pl.ds(pl.multiple_of(half * HALF, HALF), HALF)
        loads.append([local(grads.at[pl.ds(a, 4), :, cols], g.at[n, pl.ds(a, 4)]) for a in range(0, OUTER, 4)])
        if n == 0:
            small = [local(signs_hbm, signs), local(exps_hbm, exps)]

    peers = [*xpeer.values(), zpeer, cpeer, zcpeer]
    barrier = pltpu.get_barrier_semaphore()
    for peer in peers:
        pl.semaphore_signal(barrier, inc=1, device_id=peer, device_id_type=MESH)
    axes = [(yy, later_y), (zh, later)]
    for at, others in axes:
        for j in others:

            @pl.when(at + j < 4)
            def greet_later(others=others, j=j):
                for peer in others[j]:
                    pl.semaphore_signal(barrier, inc=1, device_id=peer, device_id_type=MESH)

    def enter():
        pl.semaphore_wait(barrier, len(peers) + (4 * yy + 4 * zh if nt > 1 else 0))
        for n, (at, others) in enumerate(axes):
            for j in others:

                @pl.when(at + j >= 4)
                def answer_earlier(others=others, j=j, n=n):
                    for peer in others[j]:
                        pl.semaphore_signal(entered.at[n], inc=1, device_id=peer, device_id_type=MESH)

    def await_later(n):
        if nt > 1:
            at = axes[n][0]

            @pl.when(at < 3)
            def _():
                pl.semaphore_wait(entered.at[n], 12 - 4 * at)

    sent = []

    def remote(src, dst, peer):
        i = len(sent)
        copy = pltpu.make_async_remote_copy(
            src_ref=src, dst_ref=dst, send_sem=ss.at[i], recv_sem=rs.at[i], device_id=peer, device_id_type=MESH
        )
        copy.start()
        sent.append(copy)
        return copy

    table, diagonal = inner_table()
    for copy in small:
        copy.wait()

    def sign_row(a):
        both = [signs[2 * a + i : 2 * a + i + 1, :] for i in (0, 1)]
        return (2 * jnp.concatenate(both, axis=1) - 1).astype(f32)

    def inner_pass(n):
        for a in range(OUTER):
            if a % 4 == 0:
                loads[n][a // 4].wait()
            y[n, a] = jnp.dot(table * sign_row(a).astype(bf16), g[n, a], preferred_element_type=f32)

    def outer_pass(k, n, half, dst, other=None):
        tile, part = CHUNKS[k]
        e = exps[0, 2 * half + tile]
        top = jnp.float32(0.0)
        for power in range(-4, 2):
            top = jnp.where(e == power, jnp.float32(4.0 * 2.0**power), top)
        lanes = pl.ds(tile * LANES, LANES)

        def one(i, carry):
            rows = pl.ds(pl.multiple_of(i * 32 + part * 16, 16), 16)
            values = hadamard_values([y[n, a, rows, lanes] for a in range(OUTER)])
            for a in range(OUTER):
                q = jnp.clip(values[a], -top, top).astype(bf16)
                at = (k, a, i // 2, i % 2)
                dst[at] = q if other is None else q + other[at]
            return carry

        lax.fori_loop(0, 8, one, 0)

    inner_pass(0)
    ks = range(len(CHUNKS))
    n2 = OUTER - NA
    left, right, far = xo[3], xo[1], xo[2]
    to_right, to_left = xpeer[1], xpeer[3]
    c_ = {}
    a1 = pl.ds(0, NA)

    def split(k):
        n = (n2 + 1 - k % 2) // 2
        return n, pl.ds(0, n), pl.ds(n, n2 - n)

    def wait(k, *names):
        for name in names:
            c_[name, k].wait_recv()

    def wide(ref, *at):
        return ref[at].astype(f32)

    def other_columns(k):
        outer_pass(k, 0, oc, qp)
        if k == 0:
            enter()
        c_["pair", k] = remote(qp.at[k], pr.at[k], cpeer)

    def own_columns(k):
        wait(k, "pair")
        outer_pass(k, 1, c, p, pr)
        c_["tR", k] = remote(p.at[k, a1, far, z], rt.at[k, 0], to_right)
        c_["tL", k] = remote(p.at[k, a1, far, oz], rt.at[k, 1], to_left)

    def z_first(k):
        c_["z2", k] = remote(p.at[k, pl.ds(NA, n2), :, oz], rz2.at[k], zpeer)

    def x_direct(k):
        c_["dR", k] = remote(p.at[k, a1, right, oz], rd.at[k, 0], to_right)
        c_["dL", k] = remote(p.at[k, a1, left, z], rd.at[k, 1], to_left)

    def x_second(k):
        wait(k, "tR")
        for a in range(NA):
            t1[k, 0, a] = rt[k, 0, a] + p[k, a, right, z]
        c_["xR", k] = remote(t1.at[k, 0], rx.at[k, 0], to_right)
        wait(k, "tL")
        for a in range(NA):
            t1[k, 1, a] = rt[k, 1, a] + p[k, a, left, oz]
        c_["xL", k] = remote(t1.at[k, 1], rx.at[k, 1], to_left)

    def z_then_x(k):
        wait(k, "z2")
        n, upper, lower = split(k)
        for j in (2, 1, 3):
            for a in range(n2):
                d[k, j - 1, a] = p[k, NA + a, xo[j], z] + rz2[k, a, xo[j]]
            if j == 2:
                c_["uR", k] = remote(d.at[k, 1, upper], ru.at[k, upper], to_right)
                c_["uL", k] = remote(d.at[k, 1, lower], ru.at[k, lower], to_left)
        c_["eR", k] = remote(d.at[k, 0, lower], re.at[k, lower], to_right)
        c_["eL", k] = remote(d.at[k, 2, upper], re.at[k, upper], to_left)

    def x_then_z(k):
        wait(k, "dR", "xL")
        for a in range(NA):
            s1[k, a] = (wide(p, k, a, x, oz) + wide(rd, k, 0, a) + wide(rx, k, 1, a)).astype(bf16)
        c_["z1", k] = remote(s1.at[k], rz1.at[k], zpeer)

    def x_second_after_z(k):
        n, upper, lower = split(k)
        wait(k, "uR")
        for a in range(n):
            t2[k, a] = ru[k, a] + d[k, 0, a]
        c_["vR", k] = remote(t2.at[k, upper], rv.at[k, upper], to_right)
        wait(k, "uL")
        for a in range(n, n2):
            t2[k, a] = ru[k, a] + d[k, 2, a]
        c_["vL", k] = remote(t2.at[k, lower], rv.at[k, lower], to_left)

    def place(k, a, x, h):
        tile, part = CHUNKS[k]
        return gv.at[2 * c + tile, a, x, h, pl.ds(part * 16, 16)]

    every, first, last = pl.ds(0, OUTER), pl.ds(0, OUTER // 2), pl.ds(OUTER // 2, OUTER // 2)
    ga, gb = pl.ds(0, NG), pl.ds(NG, OUTER - NG)
    ga_first, ga_last = pl.ds(0, NG // 2), pl.ds(NG // 2, NG - NG // 2)

    def pass_on(name, k, a, x, h, peer):
        c_[name, k] = remote(place(k, a, x, h), place(k, a, x, h), peer)

    def to_core(name, k, x):
        tile, part = CHUNKS[k]
        block = gv.at[2 * c + tile, :, x, :, pl.ds(part * 16, 16)]
        c_[name, k] = remote(block, block, cpeer)

    squares = []

    def own_rows(k):
        wait(k, "dL", "xR", "eR", "eL", "vR", "vL", "z1")
        values, square = [], jnp.zeros((16, LANES), f32)
        for a in range(OUTER):
            total = wide(p, k, a, x, z)
            if a < NA:
                total = total + wide(rd, k, 1, a) + wide(rx, k, 0, a) + wide(rz1, k, a)
            else:
                total = total + wide(rz2, k, a - NA, x) + wide(re, k, a - NA) + wide(rv, k, a - NA)
            square = square + total * total
            values.append(total)
        squares.append(square)
        values = hadamard_values(values)
        for a in range(OUTER):
            ov[k, a] = values[a].astype(bf16)
        here = place(k, every, x, z)
        c_["oz", k] = remote(ov.at[k], here, zpeer)
        c_["oR", k] = remote(ov.at[k], here, to_right)
        c_["oL", k] = remote(ov.at[k], here, to_left)
        c_["own", k] = local(ov.at[k], here)

    def gather_z(k):
        wait(k, "oz")
        pass_on("rR", k, ga, x, oz, to_right)
        pass_on("rL", k, ga, x, oz, to_left)

    def core_own(k):
        c_["own", k].wait()
        to_core("c1", k, x)

    def gather_x(k):
        wait(k, "oR")
        pass_on("fR", k, first, left, z, to_right)
        wait(k, "oL")
        pass_on("fL", k, last, right, z, to_left)

    def gather_x_z(k):
        pass_on("qa", k, gb, left, z, zpeer)
        pass_on("qb", k, gb, right, z, zpeer)

    def gather_x_second(k):
        wait(k, "rR")
        pass_on("hR", k, ga_first, left, oz, to_right)
        wait(k, "rL")
        pass_on("hL", k, ga_last, right, oz, to_left)

    def gather_far_z(k):
        wait(k, "fL")
        pass_on("qc", k, gb, far, z, zpeer)

    def core_near(k):
        wait(k, "qa")
        to_core("c2", k, left)
        wait(k, "qb")
        to_core("c3", k, right)

    def core_far(k):
        wait(k, "fR", "hR", "hL", "qc")
        to_core("c4", k, far)

    ar_copies = []
    ar_round = 0

    def sum_round():
        nonlocal ar_round
        n = ar_round
        ar_round += 1
        if n == 0:
            total = functools.reduce(lambda u, v: u + v, squares)
            total = jnp.sum(total, axis=0, keepdims=True)
        else:
            for copy in ar_copies:
                copy.wait_recv()
            slots = len(rounds[n - 1][1]) + 1
            total = functools.reduce(lambda u, v: u + v, [ar[n - 1, i] for i in range(slots)])
        if n == len(rounds):
            return total
        slot, to = rounds[n]
        ar[n, slot] = total
        await_later(n)
        ar_copies[:] = [remote(ar.at[n, slot], ar.at[n, slot], peer) for peer in to]
        return None

    drained = 0

    def drain(upto):
        nonlocal drained
        for copy in sent[drained:upto]:
            copy.wait_send()
        drained = upto

    steps = dict(
        vp=other_columns,
        vo=own_columns,
        sd=x_direct,
        sz=z_first,
        a1s2=x_second,
        a2s1=z_then_x,
        a1z=x_then_z,
        a2s2=x_second_after_z,
        fin=own_rows,
        g1=gather_z,
        gc1=core_own,
        g2f=gather_x,
        g2q=gather_x_z,
        g3=gather_x_second,
        g4=gather_far_z,
        g5=core_near,
        g6=core_far,
    )
    total, weight_load, mark = None, None, 0
    for step in ORDER:
        name, k = step.split()
        if name == "inner":
            inner_pass(1)
        elif name == "tables":
            weight_load = local(weights, wv)
            for a in range(OUTER):
                signed = jnp.where(diagonal, jnp.broadcast_to(sign_row(a), (INNER, INNER)), 0.0).astype(bf16)
                hb[a] = jnp.dot(signed, table, preferred_element_type=f32).astype(bf16)
        elif name == "sum":
            got = sum_round()
            total = total if got is None else got
        elif name == "drain":
            drain(mark)
            mark = len(sent)
        else:
            steps[name](int(k))

    total = jnp.sum(total, axis=1, keepdims=True)
    factor = 0.5 / jnp.sqrt(total / (OUTER * INNER * COLS) + 1e-06)
    fac[...] = jnp.broadcast_to(factor, fac.shape)
    weight_load.wait()
    drain(len(sent))
    for k in ks:
        wait(k, "c1", "c2", "c3", "c4")


def finish(gv, wv, hb, fac, out, stage, sem):
    f32 = jnp.float32
    factor = fac[0:1, 0:1]
    copies = []
    for a in range(OUTER):
        block = jnp.concatenate([gv[i, a].reshape(INNER, LANES) for i in range(4)], axis=1)
        unrotated = jnp.dot(hb[a], block, preferred_element_type=f32)
        stage[a] = (wv[a].astype(f32) - factor * unrotated).astype(stage.dtype)
        copies.append(pltpu.make_async_copy(stage.at[a], out.at[a], sem.at[a]))
        copies[-1].start()
    for copy in copies:
        copy.wait()


def body(exponents, signs, grads, weights, nt):
    bf16, f32 = jnp.bfloat16, jnp.float32
    n_copies = 31 * len(CHUNKS) + 2 * (15 if nt > 1 else 3)
    vmem = pltpu.VMEM
    columns = grads.shape[-1]
    nk, na2 = len(CHUNKS), OUTER - NA
    chunk = (nk, OUTER, 4, 2, 16, LANES)
    any_, in_vmem = pl.BlockSpec(memory_space=pl.ANY), pl.BlockSpec(memory_space=pltpu.VMEM)
    gv, wv, hb, fac = pl.pallas_call(
        functools.partial(exchange, nt),
        out_shape=[
            vmem((4, OUTER, 4, 2, 32, LANES), bf16),
            vmem((OUTER, INNER, columns), bf16),
            vmem((OUTER, INNER, INNER), bf16),
            vmem((8, LANES), f32),
        ],
        in_specs=[any_] * 4,
        out_specs=[in_vmem] * 4,
        scratch_shapes=[
            pltpu.SMEM((1, 4), jnp.int32),
            vmem((32, LANES), jnp.int32),
            vmem((2, OUTER, INNER, HALF), bf16),
            vmem((2, OUTER, INNER, HALF), f32),
            vmem(chunk, bf16),
            vmem(chunk, bf16),
            vmem(chunk, bf16),
            vmem((nk, 2, NA, 16, LANES), bf16),
            vmem((nk, 2, NA, 16, LANES), bf16),
            vmem((nk, 2, NA, 16, LANES), bf16),
            vmem((nk, 2, NA, 16, LANES), bf16),
            vmem((nk, NA, 16, LANES), bf16),
            vmem((nk, NA, 16, LANES), bf16),
            vmem((nk, na2, 4, 16, LANES), bf16),
            vmem((nk, 3, na2, 16, LANES), bf16),
            vmem((nk, na2, 16, LANES), bf16),
            vmem((nk, na2, 16, LANES), bf16),
            vmem((nk, na2, 16, LANES), bf16),
            vmem((nk, na2, 16, LANES), bf16),
            vmem((nk, OUTER, 16, LANES), bf16),
            vmem((2, 16, 1, LANES), f32),
            pltpu.SemaphoreType.DMA((16,)),
            pltpu.SemaphoreType.DMA((n_copies,)),
            pltpu.SemaphoreType.DMA((n_copies,)),
            pltpu.SemaphoreType.REGULAR((2,)),
        ],
        compiler_params=pltpu.CompilerParams(
            collective_id=0, has_side_effects=True, vmem_limit_bytes=30 * 2**20
        ),
        name="average_step",
    )(
        pltpu.with_memory_space_constraint(exponents, pltpu.HBM),
        pltpu.with_memory_space_constraint(signs.reshape(32, LANES), pltpu.HBM),
        pltpu.with_memory_space_constraint(grads.reshape(OUTER, INNER, columns), pltpu.HBM),
        pltpu.with_memory_space_constraint(weights.reshape(OUTER, INNER, columns), pltpu.HBM),
    )
    out = pl.pallas_call(
        finish,
        out_shape=jax.ShapeDtypeStruct((OUTER, INNER, columns), bf16),
        in_specs=[in_vmem] * 4,
        out_specs=any_,
        scratch_shapes=[vmem((OUTER, INNER, columns), bf16), pltpu.SemaphoreType.DMA((OUTER,))],
        compiler_params=pltpu.CompilerParams(vmem_limit_bytes=24 * 2**20),
        name="finish_step",
    )(gv, wv, hb, fac)
    return out.reshape(OUTER * INNER, columns)


def solution(mesh):
    in_specs = (P("replica", None, "tensor"), P("replica", "tensor"), P(), P(None, "tensor"))
    nt = mesh.shape["tensor"]

    def step(grads, exponents, signs, weights):
        return body(exponents, signs, grads[0], weights, nt)

    return jax.shard_map(step, mesh=mesh, in_specs=in_specs, out_specs=P(None, "tensor"), check_vma=False)
```
